32 devices in a mesh: tm: 8 (over z, x), lat: 4 (over y, core).
Axes of the slice: x: 2, y: 2, z: 4, core: 2. Of those that a mesh axis runs over, the one named last changes fastest.
Arguments:
- wind_east: bfloat16 [960, 32, 1440], P('tm', 'lat'), may hold values from -40 to 40
- wind_north: bfloat16 [960, 32, 1440], P('tm', 'lat'), may hold values from -40 to 40
- snap_counts: int32 [8], P('tm'), may hold values from 1 to 120, 320 in all
- snap_ids: int32 [960], P('tm'), may hold values from 0 to 8759
Outputs:
- basis: bfloat16 [32, 32, 1440], P(None, 'lat')
- coeffs: float32 [32, 960], P(None, 'tm')
The draws below stay inside these ranges and needn't reach their ends.
Inputs may be any that keep to these rules, and one draw needn't show every extreme that they name: `snap_counts`: entry b counts the used slots of the b-th block of 120 slots, which are that block's first ones; the entries sum to 320 and one of them equals 120.
All inputs are finite; a program needn't handle non-finite values.
Results may differ from the reference program's by a relative error of at most 0.0072.
Values may be sent and summed in bfloat16 or wider, within the bound.
No kernel may reach another device: no remote copies, remote signals or barrier semaphores. Data moves between devices by JAX's collectives and lax.ppermute only.
A program may use at most 64 MiB of HBM per device.

```python
import math
import jax
import jax.numpy as jnp
import numpy as np
from jax import lax

NLON = 1440
RANK = 32
SNAP_MAX = 120
SNAP_MEAN = 40
NLAT = 32
SNAPS = 960
CELLS = 46080
N_TM = 8


def wind_field(key, salt):
    keys = jax.random.split(jax.random.fold_in(key, salt), 5)
    modes = jax.random.normal(keys[0], (4, NLAT, NLON), jnp.float32)
    amplitude = jax.random.normal(keys[1], (SNAPS, 4), jnp.float32)
    noise = jax.random.normal(keys[2], (SNAPS, NLAT, NLON), jnp.float32)
    common = 0.5
    shared = jnp.einsum('sk,kab->sab', amplitude, modes)
    base = (common * shared + noise) / jnp.sqrt(1.0 + 4.0 * common * common)
    row_place = jnp.arange(NLAT, dtype=jnp.float32) / NLAT
    row_scale = 10.0 ** (0.5 * row_place + 0.5 * jax.random.uniform(keys[3], (NLAT,), jnp.float32)) / jnp.sqrt(10.0)
    snap_scale = 10.0 ** (jax.random.uniform(keys[4], (SNAPS,), jnp.float32) - 0.5)
    values = base * row_scale[None, :, None] * snap_scale[:, None, None]
    return jnp.clip(values, -40.0, 40.0)


def draw_wind_east(key, part):
    return wind_field(key, 11).astype(jnp.bfloat16)


def draw_wind_north(key, part):
    return wind_field(key, 23).astype(jnp.bfloat16)


def with_ends(drawn, own_key, low, top_value):
    shape = drawn.shape
    spot = [jax.random.randint(jax.random.fold_in(own_key, axis), (), 0, shape[axis]) for axis in range(len(shape))]
    drawn = drawn.at[tuple(spot)].set(low)
    longest = shape.index(max(shape))
    spot[longest] = (spot[longest] + 1) % shape[longest]
    return drawn.at[tuple(spot)].set(top_value)


def length_profile(number_of, total, reach, slope):
    portions = [(1 << 20) // math.isqrt(grade ** slope) + 1 for grade in range(2, number_of + 1)]
    spare, holding = total - reach - (number_of - 1), [1] * (number_of - 1)
    while spare > 0:
        candidates = [i for i in range(number_of - 1) if holding[i] < reach]
        whole, budget = sum([portions[i] for i in candidates]), spare
        for i in candidates:
            more = min(reach - holding[i], max(1, budget * portions[i] // whole), spare)
            holding[i] = holding[i] + more
            spare = spare - more
    return np.array([reach] + holding)


def uneven(key, number_of, total, reach, slope):
    if number_of == 2:
        one = jax.random.randint(key, (), max(1, total - reach), min(reach, total - 1) + 1)
        return jnp.stack([one, total - one])
    lengths = jnp.asarray(length_profile(number_of, total, reach, slope), jnp.int32)
    couples = (number_of - 1) // 2
    source_of, sink = lengths[1:1 + 2 * couples:2], lengths[2:2 + 2 * couples:2]
    margin = jnp.minimum(source_of - 1, reach - sink)
    shifted = jax.random.randint(jax.random.fold_in(key, 1), (couples,), 0, 1 << 20) % (margin + 1)
    lengths = lengths.at[1:1 + 2 * couples:2].set(source_of - shifted).at[2:2 + 2 * couples:2].set(sink + shifted)
    return lengths[jax.random.permutation(jax.random.fold_in(key, 2), number_of)]


def setup_inputs(seed: int = 0) -> dict:
    key_list = jax.random.split(jax.random.key(seed), 5)
    return {
        "wind_east": draw_wind_east(jax.random.fold_in(key_list[4], 71), 0),
        "wind_north": draw_wind_north(jax.random.fold_in(key_list[4], 71), 0),
        "snap_counts": uneven(key_list[2], N_TM, SNAP_MEAN * N_TM, SNAP_MAX, 2).astype(jnp.int32),
        "snap_ids": with_ends(jax.random.randint(key_list[3], (SNAPS,), 0, 8760), jax.random.fold_in(key_list[3], 1), 0, 8759).astype(jnp.int32),
    }


def latitude_cosine(first_row, row_count, total_rows):
    row_index = first_row + jnp.arange(row_count, dtype=jnp.int32)
    return jnp.cos((total_rows // 2 - row_index).astype(jnp.float32) * (jnp.pi / 720.0))

def sign_table(snap_ids, rank_count):
    column = jnp.arange(rank_count, dtype=jnp.int32)
    mixed = snap_ids[:, None] * 1103515245 + column[None, :] * 40503 + 12345
    mixed = jnp.bitwise_xor(mixed, jnp.right_shift(mixed, 13))
    mixed = mixed * 1664525 + 1013904223
    mixed = jnp.bitwise_xor(mixed, jnp.right_shift(mixed, 16))
    flipped = jnp.bitwise_and(jnp.right_shift(mixed, 7), 1)
    return (1 - 2 * flipped).astype(jnp.bfloat16)

def metric_vorticity(padded_east, wind_north, padded_cosine, valid):
    scaled = padded_east.astype(jnp.float32) * padded_cosine[None, :, None]
    north_side = scaled[:, :-2]
    south_side = scaled[:, 2:]
    meridional = wind_north.astype(jnp.float32)
    zonal_diff = jnp.roll(meridional, -1, axis=2) - jnp.roll(meridional, 1, axis=2)
    weight = 0.5 / jnp.sqrt(padded_cosine[1:-1])
    field = (zonal_diff - north_side + south_side) * weight[None, :, None] * valid[:, None, None]
    return field.astype(jnp.bfloat16)

def reference(wind_east, wind_north, snap_counts, snap_ids):
    slot_index = jnp.arange(SNAPS, dtype=jnp.int32)
    valid_all = (slot_index % SNAP_MAX < snap_counts[slot_index // SNAP_MAX]).astype(jnp.float32)
    padded_cosine = latitude_cosine(-1, NLAT + 2, NLAT)
    signs_all = sign_table(snap_ids, RANK)
    east_blocks = wind_east.reshape(N_TM, SNAP_MAX, NLAT, NLON)
    north_blocks = wind_north.reshape(N_TM, SNAP_MAX, NLAT, NLON)
    valid_blocks = valid_all.reshape(N_TM, SNAP_MAX)
    sign_blocks = signs_all.reshape(N_TM, SNAP_MAX, RANK)

    def block_field(block):
        padded = jnp.pad(east_blocks[block], ((0, 0), (1, 1), (0, 0)))
        field = metric_vorticity(padded, north_blocks[block], padded_cosine, valid_blocks[block])
        return field.reshape(SNAP_MAX, NLAT * NLON)

    def accumulate(total, block):
        field = block_field(block)
        return (total + jnp.dot(sign_blocks[block].T.astype(jnp.float32), field.astype(jnp.float32), preferred_element_type=jnp.float32), None)
    block_list = jnp.arange(N_TM, dtype=jnp.int32)
    sketch, _ = lax.scan(accumulate, jnp.zeros((RANK, NLAT * NLON), jnp.float32), block_list)
    gram_sum = lax.dot_general(sketch.astype(jnp.float32), sketch.astype(jnp.float32), (((1,), (1,)), ((), ())), precision=lax.Precision.HIGHEST, preferred_element_type=jnp.float32) / CELLS
    factor = jnp.linalg.cholesky(gram_sum)
    inverse = lax.linalg.triangular_solve(factor, jnp.eye(RANK, dtype=jnp.float32), left_side=True, lower=True)
    basis_flat = jnp.dot(inverse.astype(jnp.float32), sketch.astype(jnp.float32), precision=lax.Precision.HIGHEST, preferred_element_type=jnp.float32).astype(jnp.bfloat16)

    def project(block):
        field = block_field(block)
        return lax.dot_general(basis_flat.astype(jnp.float32), field.astype(jnp.float32), (((1,), (1,)), ((), ())), preferred_element_type=jnp.float32) / CELLS
    projected = lax.map(project, block_list)
    coeffs = jnp.transpose(projected, (1, 0, 2)).reshape(RANK, SNAPS)
    return (basis_flat.reshape(RANK, NLAT, NLON), coeffs)
```

```python
import functools

import jax
import jax.numpy as jnp
from jax import lax
from jax.experimental import pallas as pl
from jax.experimental.pallas import tpu as pltpu
from jax.sharding import PartitionSpec as P

RANK = 32
VMEM_LIMIT = 48 * 1024 * 1024
HIGHEST = lax.Precision.HIGHEST
WHOLE = pl.BlockSpec(memory_space=pltpu.VMEM)
SCALARS = pl.BlockSpec(memory_space=pltpu.SMEM)


def params():
    return pltpu.CompilerParams(vmem_limit_bytes=VMEM_LIMIT)


def mm(a, b, dims=((1,), (0,)), precision=None):
    return lax.dot_general(a, b, (dims, ((), ())), precision=precision, preferred_element_type=jnp.float32)


def iota(shape, axis):
    return lax.broadcasted_iota(jnp.int32, shape, axis)


def one_hot(condition):
    return condition.astype(jnp.float32).astype(jnp.bfloat16)


def pick_rows(value, rows, j):
    shape = (RANK, value.shape[0])
    return mm(one_hot(iota(shape, 1) == iota(shape, 0) * rows + j), value)


def padded_width(lon_count):
    return lon_count if lon_count % 128 == 0 else (lon_count + 2 + 127) // 128 * 128


def lon_shifts(value, lon_count):
    width = value.shape[1]
    return pltpu.roll(value, width - 1, 1), pltpu.roll(value, 1, 1)


def wrap_columns(ref, lon_count):
    width = ref.shape[1]
    if width != lon_count:
        ref[:, lon_count : lon_count + 1] = ref[:, 0:1]
        ref[:, width - 1 : width] = ref[:, lon_count - 1 : lon_count]


def sketch_kernel(
    rows, chunk, lon_count, scal_ref, ids_ref, coef_ref, east_ref, north_ref, main_ref, up_ref, down_ref,
    signs_ref, se_ref, sw_ref
):
    step = pl.program_id(0)
    slots = ids_ref.shape[1]
    per_piece = scal_ref[2]
    wide = RANK * rows

    @pl.when(step == 0)
    def _():
        order = iota((RANK, slots), 0)
        column = jnp.bitwise_xor(scal_ref[0], order // per_piece) * per_piece + order % per_piece
        mixed = ids_ref[...] * 1103515245 + column * 40503 + 12345
        mixed = jnp.bitwise_xor(mixed, jnp.right_shift(mixed, 13))
        mixed = mixed * 1664525 + 1013904223
        mixed = jnp.bitwise_xor(mixed, jnp.right_shift(mixed, 16))
        flipped = jnp.bitwise_and(jnp.right_shift(mixed, 7), 1)
        used = iota((RANK, slots), 1) < scal_ref[1]
        signs = jnp.where(used, 1 - 2 * flipped, 0).astype(jnp.float32).astype(jnp.bfloat16)
        spread = one_hot(iota((wide, RANK), 0) // rows == iota((wide, RANK), 1))
        tall = mm(spread, signs).astype(jnp.bfloat16)
        across = one_hot(iota((slots, slots * rows), 1) // rows == iota((slots, slots * rows), 0))
        full = mm(tall, across)
        same = iota(full.shape, 0) % rows == iota(full.shape, 1) % rows
        signs_ref[...] = jnp.where(same, full, 0.0).astype(jnp.bfloat16)

    place = pl.ds(pl.multiple_of(step * chunk, 128), chunk)
    se_ref[:, place] = mm(signs_ref[...], east_ref[...])
    sw_ref[:, place] = mm(signs_ref[...], north_ref[...])

    @pl.when(step == pl.num_programs(0) - 1)
    def _():
        wrap_columns(sw_ref, lon_count)
        rounded = se_ref[:, :lon_count].astype(jnp.bfloat16)
        up_ref[...] = pick_rows(rounded, rows, rows - 1).astype(jnp.bfloat16)
        down_ref[...] = pick_rows(rounded, rows, 0).astype(jnp.bfloat16)
        band = 4 * rows

        def body(index, carry):
            at = pl.ds(pl.multiple_of(index * band, band), band)
            ahead, behind = lon_shifts(sw_ref[at, : padded_width(lon_count)], lon_count)
            east = se_ref[at, : padded_width(lon_count)]
            north_side = pltpu.roll(east, 1, 0)
            south_side = pltpu.roll(east, band - 1, 0)
            total = (
                (ahead - behind) * coef_ref[at, 0:1]
                + north_side * coef_ref[at, 1:2]
                + south_side * coef_ref[at, 2:3]
            )
            main_ref[at, :] = total[:, :lon_count]
            return carry

        lax.fori_loop(0, RANK * rows // band, body, 0)


def halo_kernel(rows, scal_ref, coef_ref, main_ref, up_ref, down_ref, send_ref, keep_ref):
    per_piece = scal_ref[2]
    wide = RANK * rows
    half = wide // 2

    def real(order, me):
        return jnp.bitwise_xor(me, order // per_piece) * per_piece + order % per_piece

    row = iota((wide, RANK), 0)
    mine = real(row // rows, scal_ref[0])
    north_place = one_hot((mine == real(iota((wide, RANK), 1), scal_ref[3])) & (row % rows == 0))
    south_place = one_hot((mine == real(iota((wide, RANK), 1), scal_ref[3])) & (row % rows == rows - 1))
    total = main_ref[...] + coef_ref[:, 3:4] * (mm(north_place, up_ref[...]) + mm(south_place, down_ref[...]))
    keep_ref[...] = total[:half]
    send_ref[...] = total[half:].astype(jnp.bfloat16)


def project_kernel(
    rows, lon_count, piece_count, scal_ref, coef_ref, *refs
):
    piece_refs = refs[:piece_count]
    (up_ref, down_ref, east_ref, north_ref, sketch_ref, sums_ref, work, to_east, to_north, slots_ref) = refs[piece_count:]
    step = pl.program_id(0)
    wide = RANK * rows
    per_piece = scal_ref[2]
    piece_rows = RANK * rows // scal_static(piece_refs)
    fold = one_hot(iota((RANK, wide), 1) // rows == iota((RANK, wide), 0))

    @pl.when(step == 0)
    def _():
        start = 0
        for ref in piece_refs:
            for inner in range(ref.shape[0] // piece_rows):
                owner = jnp.bitwise_xor(scal_ref[0], start)
                at = pl.ds(pl.multiple_of(owner * piece_rows, piece_rows), piece_rows)
                sketch_ref[at, :] = ref[inner * piece_rows : (inner + 1) * piece_rows, :]
                start += 1
        work[:, :lon_count] = sketch_ref[...].astype(jnp.float32)
        wrap_columns(work, lon_count)
        band = 4 * rows

        def body(index, carry):
            at = pl.ds(pl.multiple_of(index * band, band), band)
            value = work[at, :]
            ahead, behind = lon_shifts(value, lon_count)
            to_north[at, :] = ((behind - ahead) * coef_ref[at, 0:1])[:, :lon_count].astype(jnp.bfloat16)
            above = pltpu.roll(value, 1, 0)
            below = pltpu.roll(value, band - 1, 0)
            to_east[at, :] = (above * coef_ref[at, 4:5] + below * coef_ref[at, 5:6])[:, :lon_count].astype(jnp.bfloat16)
            return carry

        lax.fori_loop(0, RANK * rows // band, body, 0)

    both = mm(east_ref[...], to_east[...], ((1,), (1,))) + mm(north_ref[...], to_north[...], ((1,), (1,)))
    same = iota(both.shape, 0) % rows == iota(both.shape, 1) % rows
    slots = both.shape[0] // rows
    summed = jnp.sum(jnp.where(same, both, 0.0).reshape(slots, rows, wide), axis=1)
    slots_ref[pl.ds(pl.multiple_of(step * slots, slots), slots), :] = summed

    @pl.when(step == pl.num_programs(0) - 1)
    def _():
        value = sketch_ref[...]
        gram = mm(value, value, ((1,), (1,)))
        same = iota(gram.shape, 0) % rows == iota(gram.shape, 1) % rows
        gram = jnp.sum(jnp.where(same, gram, 0.0).reshape(RANK, rows, wide), axis=1)
        gram = mm(gram, fold.astype(jnp.float32), ((1,), (1,)), HIGHEST)
        terms = mm(fold.astype(jnp.float32), slots_ref[...], ((1,), (1,)), HIGHEST)
        first = pick_rows(value, rows, 0)
        last = pick_rows(value, rows, rows - 1)
        first = (first * coef_ref[0:1, 3:4]).astype(jnp.bfloat16)
        last = (last * coef_ref[rows - 1 : rows, 3:4]).astype(jnp.bfloat16)
        terms += mm(first, up_ref[...], ((1,), (1,))) + mm(last, down_ref[...], ((1,), (1,)))
        width = terms.shape[1]
        sums_ref[...] = jnp.zeros_like(sums_ref)
        sums_ref[:, :width] = terms
        sums_ref[:, sums_ref.shape[1] - 128 : sums_ref.shape[1] - 128 + RANK] = gram


def scal_static(piece_refs):
    return sum(ref.shape[0] for ref in piece_refs) // piece_refs[0].shape[0]


def solve_kernel(rows, cell_total, scal_ref, sums_ref, sketch_ref, basis_ref, coeffs_ref, work):
    scale = 1.0 / cell_total
    slots = coeffs_ref.shape[1]
    wide = RANK * rows
    offset = sums_ref.shape[1] - 128
    work[...] = jnp.zeros_like(work)
    gram = sums_ref[:, offset : offset + RANK] * scale
    row, column = iota((RANK, RANK), 0), iota((RANK, RANK), 1)
    work[:, :RANK] = gram
    work[:, RANK : 2 * RANK] = (row == column).astype(jnp.float32)
    table = work[...]
    down, along = iota(table.shape, 0), iota(table.shape, 1)
    for k in range(RANK):
        pivot_row = table[k : k + 1, :]
        pivot = table[k : k + 1, k : k + 1]
        factor = jnp.where(down[:, 0:1] > k, table[:, k : k + 1] / pivot, 0.0)
        table = table - factor * pivot_row
    diagonal = jnp.sum(jnp.where(down == along, table, 0.0), axis=1, keepdims=True)
    work[...] = table * (1.0 / jnp.sqrt(diagonal))
    inverse = work[:, RANK : 2 * RANK]
    raw = mm(inverse, sums_ref[:, :slots], precision=HIGHEST) * scale
    coeffs_ref[...] = jnp.where(iota(raw.shape, 1) < scal_ref[1], raw, 0.0)
    spread = (iota((wide, RANK), 0) // rows == iota((wide, RANK), 1)).astype(jnp.float32)
    tall = mm(spread, inverse, precision=HIGHEST)
    large = mm(tall, spread, ((1,), (1,)), HIGHEST)
    same = iota(large.shape, 0) % rows == iota(large.shape, 1) % rows
    large = jnp.where(same, large, 0.0)
    high = large.astype(jnp.bfloat16)
    rest = large - high.astype(jnp.float32)
    middle = rest.astype(jnp.bfloat16)
    low = (rest - middle.astype(jnp.float32)).astype(jnp.bfloat16)
    value = sketch_ref[...]
    basis_ref[...] = (mm(high, value) + (mm(middle, value) + mm(low, value))).astype(jnp.bfloat16)


def cosine(row_index, total_rows):
    return jnp.cos((total_rows // 2 - row_index).astype(jnp.float32) * (jnp.pi / 720.0))


def coefficients(first_row, rows, total_rows):
    j = jnp.arange(rows, dtype=jnp.int32)
    here = first_row + j
    def weight(row):
        return 0.5 / jnp.sqrt(cosine(row, total_rows))
    first, last = j == 0, j == rows - 1
    north = -cosine(here - 1, total_rows) * weight(here)
    south = cosine(here + 1, total_rows) * weight(here)
    columns = [
        weight(here),
        jnp.where(first, 0.0, north),
        jnp.where(last, 0.0, south),
        jnp.where(first, north, jnp.where(last, south, 0.0)),
        jnp.where(first, 0.0, cosine(here, total_rows) * weight(here - 1)),
        jnp.where(last, 0.0, -cosine(here, total_rows) * weight(here + 1)),
    ]
    table = jnp.stack(columns + [jnp.zeros_like(columns[0])] * 2, axis=1)
    return jnp.tile(table, (RANK, 1))


def bit_order(lat, bits):
    order = list(range(bits))
    if lat % 2 and bits > 1:
        order[0], order[1] = order[1], order[0]
    return order


def relative_place(tm, parity, bits):
    def place(order):
        total = 0
        for turn, bit in enumerate(order):
            total = total + (((tm >> bit) & 1) << (bits - 1 - turn))
        return total
    return jnp.where(parity == 1, place(bit_order(1, bits)), place(bit_order(0, bits)))


def partners(turn, bits, tm_count, lat_count):
    pairs = []
    for tm in range(tm_count):
        for lat in range(lat_count):
            bit = bit_order(lat, bits)[turn]
            pairs.append((tm * lat_count + lat, (tm ^ (1 << bit)) * lat_count + lat))
    return pairs


def local(wind_east, wind_north, snap_counts, snap_ids):
    slots, rows, lon_count = wind_east.shape
    tm_count, lat_count = lax.axis_size("tm"), lax.axis_size("lat")
    bits = tm_count.bit_length() - 1
    tm, lat = lax.axis_index("tm"), lax.axis_index("lat")
    wide = RANK * rows
    per_piece = RANK // tm_count
    total_rows = rows * lat_count
    cell_total = total_rows * lon_count
    width = padded_width(lon_count)
    me = relative_place(tm, lat % 2, bits)
    beside = relative_place(tm, 1 - lat % 2, bits)
    scal = jnp.stack([me, snap_counts[0], jnp.int32(per_piece), beside]).astype(jnp.int32)
    coef = coefficients(lat * rows, rows, total_rows)
    east = wind_east.reshape(slots * rows, lon_count)
    north = wind_north.reshape(slots * rows, lon_count)
    northward = [(i + 1, i) for i in range(lat_count - 1)]
    southward = [(i, i + 1) for i in range(lat_count - 1)]

    chunk = 128 * -(-width // 512)
    steps = -(-width // chunk)
    field_spec = pl.BlockSpec((slots * rows, chunk), lambda i: (0, i))
    fixed = lambda shape: pl.BlockSpec(shape, lambda i: (0,) * len(shape))
    main, up, down = pl.pallas_call(
        functools.partial(sketch_kernel, rows, chunk, lon_count),
        grid=(steps,),
        in_specs=[SCALARS, fixed((1, slots)), fixed((wide, 8)), field_spec, field_spec],
        out_specs=[fixed((wide, lon_count)), fixed((RANK, lon_count)), fixed((RANK, lon_count))],
        out_shape=[
            jax.ShapeDtypeStruct((wide, lon_count), jnp.float32),
            jax.ShapeDtypeStruct((RANK, lon_count), jnp.bfloat16),
            jax.ShapeDtypeStruct((RANK, lon_count), jnp.bfloat16),
        ],
        scratch_shapes=[
            pltpu.VMEM((wide, slots * rows), jnp.bfloat16),
            pltpu.VMEM((wide, steps * chunk), jnp.float32),
            pltpu.VMEM((wide, steps * chunk), jnp.float32),
        ],
        compiler_params=params(),
        name="sketch_terms",
    )(scal, snap_ids.reshape(1, slots), coef, east, north)

    above = lax.ppermute(up, "lat", southward)
    below = lax.ppermute(down, "lat", northward)
    send, keep = pl.pallas_call(
        functools.partial(halo_kernel, rows),
        in_specs=[SCALARS] + [WHOLE] * 4,
        out_specs=[WHOLE, WHOLE],
        out_shape=[
            jax.ShapeDtypeStruct((wide // 2, lon_count), jnp.bfloat16),
            jax.ShapeDtypeStruct((wide // 2, lon_count), jnp.float32),
        ],
        compiler_params=params(),
        name="halo_terms",
    )(scal, coef, main, above, below)

    wind_above = lax.ppermute(wind_east[:, rows - 1, :], "lat", southward)
    wind_below = lax.ppermute(wind_east[:, 0, :], "lat", northward)

    both = ("tm", "lat")
    for turn in range(bits):
        got = lax.ppermute(send, both, partners(turn, bits, tm_count, lat_count))
        keep = keep + got.astype(jnp.float32)
        if turn < bits - 1:
            half = keep.shape[0] // 2
            send, keep = keep[half:].astype(jnp.bfloat16), keep[:half]
    held = keep.astype(jnp.bfloat16)
    pieces = [held]
    for turn in reversed(range(bits)):
        got = lax.ppermute(held, both, partners(turn, bits, tm_count, lat_count))
        pieces.append(got)
        if turn:
            held = jnp.concatenate([held, got], axis=0)

    slot_chunk = max(n for n in range(8, 33, 8) if slots % n == 0) if slots % 8 == 0 else slots
    slot_steps = slots // slot_chunk
    sums_width = -(-slots // 128) * 128 + 128
    row_spec = pl.BlockSpec((slot_chunk * rows, lon_count), lambda i: (i, 0))
    sketch, sums = pl.pallas_call(
        functools.partial(project_kernel, rows, lon_count, len(pieces)),
        grid=(slot_steps,),
        in_specs=[SCALARS, fixed((wide, 8))]
        + [fixed(piece.shape) for piece in pieces]
        + [fixed((slots, lon_count))] * 2
        + [row_spec, row_spec],
        out_specs=[fixed((wide, lon_count)), fixed((RANK, sums_width))],
        out_shape=[
            jax.ShapeDtypeStruct((wide, lon_count), jnp.bfloat16),
            jax.ShapeDtypeStruct((RANK, sums_width), jnp.float32),
        ],
        scratch_shapes=[
            pltpu.VMEM((wide, width), jnp.float32),
            pltpu.VMEM((wide, lon_count), jnp.bfloat16),
            pltpu.VMEM((wide, lon_count), jnp.bfloat16),
            pltpu.VMEM((slots, wide), jnp.float32),
        ],
        compiler_params=params(),
        name="projection_terms",
    )(scal, coef, *pieces, wind_above, wind_below, east, north)

    shift = 1
    while shift < lat_count:
        sums = sums + lax.ppermute(sums, "lat", [(i, i ^ shift) for i in range(lat_count)])
        shift *= 2

    basis, coeffs = pl.pallas_call(
        functools.partial(solve_kernel, rows, cell_total),
        in_specs=[SCALARS, WHOLE, WHOLE],
        out_specs=[WHOLE, WHOLE],
        out_shape=[
            jax.ShapeDtypeStruct((wide, lon_count), jnp.bfloat16),
            jax.ShapeDtypeStruct((RANK, slots), jnp.float32),
        ],
        scratch_shapes=[pltpu.VMEM((RANK, 128), jnp.float32)],
        compiler_params=params(),
        name="basis_and_coeffs",
    )(scal, sums, sketch)
    return basis.reshape(RANK, rows, lon_count), coeffs


def solution(mesh):
    in_specs = (P("tm", "lat", None), P("tm", "lat", None), P("tm"), P("tm"))
    out_specs = (P(None, "lat", None), P(None, "tm"))
    return jax.shard_map(local, mesh=mesh, in_specs=in_specs, out_specs=out_specs, check_vma=False)
```

```python
import functools

import jax
import jax.numpy as jnp
from jax import lax
from jax.experimental import pallas as pl
from jax.experimental.pallas import tpu as pltpu
from jax.sharding import PartitionSpec as P

RANK = 32
VMEM_LIMIT = 32 * 1024 * 1024
HIGHEST = lax.Precision.HIGHEST
WHOLE = pl.BlockSpec(memory_space=pltpu.VMEM)
SCALARS = pl.BlockSpec(memory_space=pltpu.SMEM)
FAR = pl.BlockSpec(memory_space=pltpu.HBM)


def in_hbm(array):
    return pltpu.with_memory_space_constraint(array, pltpu.HBM)


def params():
    return pltpu.CompilerParams(vmem_limit_bytes=VMEM_LIMIT)


def mm(a, b, dims=((1,), (0,)), precision=None):
    return lax.dot_general(a, b, (dims, ((), ())), precision=precision, preferred_element_type=jnp.float32)


def iota(shape, axis):
    return lax.broadcasted_iota(jnp.int32, shape, axis)


def one_hot(condition):
    return jnp.where(condition, 1.0, 0.0).astype(jnp.bfloat16)


def group(count, rows, axis):
    index = iota((count, 1) if axis == 0 else (1, count), axis)
    if rows & (rows - 1) == 0:
        return jnp.right_shift(index, rows.bit_length() - 1), jnp.bitwise_and(index, rows - 1)
    return index // rows, index % rows


def spread_rows(rows):
    return one_hot(group(RANK * rows, rows, 0)[0] == iota((1, RANK), 1))


def same_place(tall, wide, rows):
    return group(tall, rows, 0)[1] == group(wide, rows, 1)[1]


def pick_rows(value, rows, j):
    return mm(one_hot(iota((1, value.shape[0]), 1) == iota((RANK, 1), 0) * rows + j), value)


def padded_width(lon_count):
    return lon_count if lon_count % 128 == 0 else (lon_count + 2 + 127) // 128 * 128


def lon_shifts(value):
    return pltpu.roll(value, value.shape[1] - 1, 1), pltpu.roll(value, 1, 1)


def wrap_columns(ref, lon_count):
    width = ref.shape[1]
    if width != lon_count:
        ref[:, lon_count : lon_count + 1] = ref[:, 0:1]
        ref[:, width - 1 : width] = ref[:, lon_count - 1 : lon_count]


def bit_order(lat, bits):
    order = list(range(bits))
    if lat % 2 and bits > 1:
        order[0], order[1] = order[1], order[0]
    return order


def relative_place(tm, parity, bits):
    def place(order):
        total = 0
        for turn, bit in enumerate(order):
            total = total + (((tm >> bit) & 1) << (bits - 1 - turn))
        return total
    return jnp.where(parity == 1, place(bit_order(1, bits)), place(bit_order(0, bits)))


def places():
    bits = lax.axis_size("tm").bit_length() - 1
    tm, parity = lax.axis_index("tm"), jnp.bitwise_and(lax.axis_index("lat"), 1)
    return relative_place(tm, parity, bits), relative_place(tm, 1 - parity, bits)


def real_column(order, place):
    per_piece = RANK // lax.axis_size("tm")
    part, inner = group(RANK, per_piece, 0 if order.shape[1] == 1 else 1)
    if order.shape[0] * order.shape[1] != RANK:
        part, inner = order // per_piece, order % per_piece
    return jnp.bitwise_xor(part, place) * per_piece + inner


def geometry(rows, repeat):
    total_rows = rows * lax.axis_size("lat")
    j = group(rows * repeat, rows, 0)[1]
    here = lax.axis_index("lat") * rows + j

    def cosine(row):
        return jnp.cos((total_rows // 2 - row).astype(jnp.float32) * (jnp.pi / 720.0))

    return j, cosine(here - 1), cosine(here), cosine(here + 1)


def weight(cosines):
    return 0.5 / jnp.sqrt(cosines)


def east_kernel(rows, lon_count, count_ref, ids_hbm, east_hbm, part_ref, up_ref, down_ref, signs_ref, ids, east, se, sems):
    slots = ids.shape[1]
    wide = RANK * rows
    cut = slots * rows // 32 * 16
    head = pltpu.make_async_copy(east_hbm.at[pl.ds(0, cut)], east.at[pl.ds(0, cut)], sems.at[0])
    tail = pltpu.make_async_copy(
        east_hbm.at[pl.ds(cut, slots * rows - cut)], east.at[pl.ds(cut, slots * rows - cut)], sems.at[1]
    )
    keys = pltpu.make_async_copy(ids_hbm, ids, sems.at[2])
    keys.start()
    head.start()
    tail.start()
    me, _ = places()
    order = iota((RANK, 1), 0)
    column = real_column(order, me)
    spread = spread_rows(rows)
    across = one_hot(group(slots * rows, rows, 1)[0] == iota((slots, 1), 0))
    j, c_north, c_here, c_south = geometry(rows, 4)
    north = jnp.where(j == 0, 0.0, -c_north * weight(c_here))
    south = jnp.where(j == rows - 1, 0.0, c_south * weight(c_here))
    keys.wait()
    mixed = ids[...] * 1103515245 + (column * 40503 + 12345)
    mixed = jnp.bitwise_xor(mixed, jnp.right_shift(mixed, 13))
    mixed = mixed * 1664525 + 1013904223
    mixed = jnp.bitwise_xor(mixed, jnp.right_shift(mixed, 16))
    flipped = jnp.bitwise_and(jnp.right_shift(mixed, 7), 1)
    used = iota((1, slots), 1) < count_ref[0]
    signs = jnp.where(used, 1 - 2 * flipped, 0).astype(jnp.float32).astype(jnp.bfloat16)
    full = mm(mm(spread, signs).astype(jnp.bfloat16), across)
    signs_ref[...] = jnp.where(same_place(wide, slots * rows, rows), full, 0.0).astype(jnp.bfloat16)
    head.wait()
    se[:, :lon_count] = mm(signs_ref[:, :cut], east[:cut, :])
    tail.wait()
    se[:, :lon_count] += mm(signs_ref[:, cut:], east[cut:, :])
    rounded = se[:, :lon_count].astype(jnp.bfloat16)
    up_ref[...] = pick_rows(rounded, rows, rows - 1).astype(jnp.bfloat16)
    down_ref[...] = pick_rows(rounded, rows, 0).astype(jnp.bfloat16)
    band = 4 * rows

    def body(index, carry):
        at = pl.ds(pl.multiple_of(index * band, band), band)
        value = se[at, :lon_count]
        part_ref[at, :] = pltpu.roll(value, 1, 0) * north + pltpu.roll(value, band - 1, 0) * south
        return carry

    lax.fori_loop(0, wide // band, body, 0)


def north_kernel(rows, lon_count, signs_ref, part_ref, north_ref, main_ref, sw):
    sw[:, :lon_count] = mm(signs_ref[...], north_ref[...])
    wrap_columns(sw, lon_count)
    scale = weight(geometry(rows, 4)[2])
    band = 4 * rows

    def body(index, carry):
        at = pl.ds(pl.multiple_of(index * band, band), band)
        ahead, behind = lon_shifts(sw[at, :])
        main_ref[at, :] = ((ahead - behind) * scale)[:, :lon_count] + part_ref[at, :]
        return carry

    lax.fori_loop(0, RANK * rows // band, body, 0)


def halo_kernel(rows, main_ref, up_ref, down_ref, send_ref, keep_ref):
    wide = RANK * rows
    half = wide // 2
    me, beside = places()
    part, j = group(wide, rows, 0)
    per_piece = RANK // lax.axis_size("tm")
    piece, inner = group(wide, rows * per_piece, 0)[0], jnp.bitwise_and(part, per_piece - 1)
    if per_piece & (per_piece - 1):
        inner = part % per_piece
    mine = jnp.bitwise_xor(piece, me) * per_piece + inner
    theirs = real_column(iota((1, RANK), 1), beside)
    _, c_north, c_here, c_south = geometry(rows, RANK)
    hit = mine == theirs
    from_north = mm(one_hot(hit & (j == 0)), up_ref[...])
    from_south = mm(one_hot(hit & (j == rows - 1)), down_ref[...])
    total = main_ref[...] + weight(c_here) * (c_south * from_south - c_north * from_north)
    keep_ref[...] = total[:half]
    send_ref[...] = total[half:].astype(jnp.bfloat16)


def project_kernel(rows, lon_count, piece_count, *refs):
    piece_refs = refs[:piece_count]
    (up_ref, down_ref, east_ref, north_ref, sketch_ref, sums_ref, work, to_east, to_north) = refs[piece_count:]
    wide = RANK * rows
    piece_rows = piece_refs[0].shape[0]
    me, _ = places()
    start = 0
    for ref in piece_refs:
        for inner in range(ref.shape[0] // piece_rows):
            owner = jnp.bitwise_xor(me, start)
            at = pl.ds(pl.multiple_of(owner * piece_rows, piece_rows), piece_rows)
            sketch_ref[at, :] = ref[inner * piece_rows : (inner + 1) * piece_rows, :]
            start += 1
    work[:, :lon_count] = sketch_ref[...].astype(jnp.float32)
    wrap_columns(work, lon_count)
    band = 4 * rows
    j, c_north, c_here, c_south = geometry(rows, 4)
    scale = weight(c_here)
    above_scale = jnp.where(j == 0, 0.0, c_here * weight(c_north))
    below_scale = jnp.where(j == rows - 1, 0.0, -c_here * weight(c_south))

    def body(index, carry):
        at = pl.ds(pl.multiple_of(index * band, band), band)
        value = work[at, :]
        ahead, behind = lon_shifts(value)
        to_north[at, :] = ((behind - ahead) * scale)[:, :lon_count].astype(jnp.bfloat16)
        mixed = pltpu.roll(value, 1, 0) * above_scale + pltpu.roll(value, band - 1, 0) * below_scale
        to_east[at, :] = mixed[:, :lon_count].astype(jnp.bfloat16)
        return carry

    lax.fori_loop(0, wide // band, body, 0)
    fold = jnp.where(group(wide, rows, 1)[0] == iota((RANK, 1), 0), 1.0, 0.0)
    both = mm(east_ref[...], to_east[...], ((1,), (1,))) + mm(north_ref[...], to_north[...], ((1,), (1,)))
    slots = both.shape[0] // rows
    both = jnp.where(same_place(both.shape[0], wide, rows), both, 0.0)
    both = jnp.sum(both.reshape(slots, rows, wide), axis=1)
    terms = mm(fold, both, ((1,), (1,)), HIGHEST)
    value = sketch_ref[...]
    gram = jnp.where(same_place(wide, wide, rows), mm(value, value, ((1,), (1,))), 0.0)
    gram = mm(jnp.sum(gram.reshape(RANK, rows, wide), axis=1), fold, ((1,), (1,)), HIGHEST)
    _, c_north, c_here, c_south = geometry(1, 1)
    top = lax.axis_index("lat") * rows
    half = rows * lax.axis_size("lat") // 2

    def cosine(row):
        return jnp.cos(jnp.full((1, 1), half - row, jnp.int32).astype(jnp.float32) * (jnp.pi / 720.0))

    first = pick_rows(value, rows, 0) * (-cosine(top - 1) * weight(cosine(top)))
    last = pick_rows(value, rows, rows - 1) * (cosine(top + rows) * weight(cosine(top + rows - 1)))
    terms += mm(first.astype(jnp.bfloat16), up_ref[...], ((1,), (1,)))
    terms += mm(last.astype(jnp.bfloat16), down_ref[...], ((1,), (1,)))
    offset = sums_ref.shape[1] - 128
    sums_ref[...] = jnp.zeros_like(sums_ref)
    sums_ref[:, : terms.shape[1]] = terms
    sums_ref[:, offset : offset + RANK] = gram


def eliminate(table, block):
    down = iota((table.shape[0], 1), 0)
    for k in range(0, RANK, block):
        columns = [jnp.broadcast_to(table[:, k + i : k + i + 1], table.shape) for i in range(block)]
        lines = [table[k + i : k + i + 1, :] for i in range(block)]
        for i in range(block):
            inverse = 1.0 / columns[i][k + i : k + i + 1, :]
            for m in range(i + 1, block):
                ratio = columns[m][k + i : k + i + 1, :] * inverse
                lines[m] = lines[m] - ratio * lines[i]
                columns[m] = columns[m] - ratio * columns[i]
            table = table - jnp.where(down > k + i, columns[i] * inverse, 0.0) * lines[i]
    return table


def solve_kernel(rows, cell_total, count_ref, sums_ref, sketch_ref, basis_ref, coeffs_ref, work):
    scale = 1.0 / cell_total
    slots = coeffs_ref.shape[1]
    wide = RANK * rows
    offset = sums_ref.shape[1] - 128
    work[...] = jnp.where(iota(work.shape, 0) + RANK == iota(work.shape, 1), 1.0, 0.0)
    work[:, :RANK] = sums_ref[:, offset : offset + RANK] * scale
    table = eliminate(work[...], 4)
    diagonal = jnp.sum(jnp.where(iota((RANK, 1), 0) == iota((1, 128), 1), table, 0.0), axis=1, keepdims=True)
    work[...] = table * (1.0 / jnp.sqrt(diagonal))
    inverse = work[:, RANK : 2 * RANK]
    spread = spread_rows(rows)
    same = same_place(wide, wide, rows)
    high = inverse.astype(jnp.bfloat16)
    rest = inverse - high.astype(jnp.float32)
    middle = rest.astype(jnp.bfloat16)
    value = sketch_ref[...]

    def apply(part):
        tall = mm(spread, part).astype(jnp.bfloat16)
        large = jnp.where(same, mm(tall, spread, ((1,), (1,))), 0.0).astype(jnp.bfloat16)
        return mm(large, value)

    basis_ref[...] = (apply(high) + apply(middle)).astype(jnp.bfloat16)
    raw = mm(inverse, sums_ref[:, :slots], precision=HIGHEST) * scale
    coeffs_ref[...] = jnp.where(iota((1, slots), 1) < count_ref[0], raw, 0.0)


def partners(turn, bits, tm_count, lat_count):
    pairs = []
    for tm in range(tm_count):
        for lat in range(lat_count):
            bit = bit_order(lat, bits)[turn]
            pairs.append((tm * lat_count + lat, (tm ^ (1 << bit)) * lat_count + lat))
    return pairs


def local(wind_east, wind_north, snap_counts, snap_ids):
    slots, rows, lon_count = wind_east.shape
    tm_count, lat_count = lax.axis_size("tm"), lax.axis_size("lat")
    bits = tm_count.bit_length() - 1
    wide = RANK * rows
    cell_total = rows * lat_count * lon_count
    width = padded_width(lon_count)
    east = wind_east.reshape(slots * rows, lon_count)
    north = wind_north.reshape(slots * rows, lon_count)
    northward = [(i + 1, i) for i in range(lat_count - 1)]
    southward = [(i, i + 1) for i in range(lat_count - 1)]
    float_array = lambda *shape: jax.ShapeDtypeStruct(shape, jnp.float32)
    half_array = lambda *shape: jax.ShapeDtypeStruct(shape, jnp.bfloat16)

    part, up, down, signs = pl.pallas_call(
        functools.partial(east_kernel, rows, lon_count),
        in_specs=[SCALARS, FAR, FAR],
        out_specs=[WHOLE] * 4,
        out_shape=[
            float_array(wide, lon_count),
            half_array(RANK, lon_count),
            half_array(RANK, lon_count),
            half_array(wide, slots * rows),
        ],
        scratch_shapes=[
            pltpu.VMEM((1, slots), jnp.int32),
            pltpu.VMEM((slots * rows, lon_count), jnp.bfloat16),
            pltpu.VMEM((wide, width), jnp.float32),
            pltpu.SemaphoreType.DMA((3,)),
        ],
        compiler_params=params(),
        name="east_terms",
    )(snap_counts, in_hbm(snap_ids.reshape(1, slots)), in_hbm(east))
    above = lax.ppermute(up, "lat", southward)
    below = lax.ppermute(down, "lat", northward)
    main = pl.pallas_call(
        functools.partial(north_kernel, rows, lon_count),
        in_specs=[WHOLE] * 3,
        out_specs=WHOLE,
        out_shape=float_array(wide, lon_count),
        scratch_shapes=[pltpu.VMEM((wide, width), jnp.float32)],
        compiler_params=params(),
        name="north_terms",
    )(signs, part, north)
    send, keep = pl.pallas_call(
        functools.partial(halo_kernel, rows),
        in_specs=[WHOLE] * 3,
        out_specs=[WHOLE, WHOLE],
        out_shape=[half_array(wide // 2, lon_count), float_array(wide // 2, lon_count)],
        compiler_params=params(),
        name="halo_terms",
    )(main, above, below)

    edge_source, send = lax.optimization_barrier((wind_east, send))
    wind_above = lax.ppermute(edge_source[:, rows - 1, :], "lat", southward)
    wind_below = lax.ppermute(edge_source[:, 0, :], "lat", northward)

    both = ("tm", "lat")
    for turn in range(bits):
        got = lax.ppermute(send, both, partners(turn, bits, tm_count, lat_count))
        if turn == min(1, bits - 1):
            got, wind_above, wind_below = lax.optimization_barrier((got, wind_above, wind_below))
        keep = keep + got.astype(jnp.float32)
        if turn < bits - 1:
            half = keep.shape[0] // 2
            send, keep = keep[half:].astype(jnp.bfloat16), keep[:half]
    held = keep.astype(jnp.bfloat16)
    pieces = [held]
    for turn in reversed(range(bits)):
        got = lax.ppermute(held, both, partners(turn, bits, tm_count, lat_count))
        pieces.append(got)
        if turn:
            held = jnp.concatenate([held, got], axis=0)

    sums_width = -(-slots // 128) * 128 + 128
    sketch, sums = pl.pallas_call(
        functools.partial(project_kernel, rows, lon_count, len(pieces)),
        in_specs=[WHOLE] * (len(pieces) + 4),
        out_specs=[WHOLE, WHOLE],
        out_shape=[half_array(wide, lon_count), float_array(RANK, sums_width)],
        scratch_shapes=[
            pltpu.VMEM((wide, width), jnp.float32),
            pltpu.VMEM((wide, lon_count), jnp.bfloat16),
            pltpu.VMEM((wide, lon_count), jnp.bfloat16),
        ],
        compiler_params=params(),
        name="projection_terms",
    )(*pieces, wind_above, wind_below, east, north)

    shift = 1
    while shift < lat_count:
        sums = sums + lax.ppermute(sums, "lat", [(i, i ^ shift) for i in range(lat_count)])
        shift *= 2

    basis, coeffs = pl.pallas_call(
        functools.partial(solve_kernel, rows, cell_total),
        in_specs=[SCALARS, WHOLE, WHOLE],
        out_specs=[WHOLE, WHOLE],
        out_shape=[half_array(wide, lon_count), float_array(RANK, slots)],
        scratch_shapes=[pltpu.VMEM((RANK, 128), jnp.float32)],
        compiler_params=params(),
        name="basis_and_coeffs",
    )(snap_counts, sums, sketch)
    return basis.reshape(RANK, rows, lon_count), coeffs


def solution(mesh):
    in_specs = (P("tm", "lat", None), P("tm", "lat", None), P("tm"), P("tm"))
    out_specs = (P(None, "lat", None), P(None, "tm"))
    return jax.shard_map(local, mesh=mesh, in_specs=in_specs, out_specs=out_specs, check_vma=False)
```

```python
import functools

import jax
import jax.numpy as jnp
from jax import lax
from jax.experimental import pallas as pl
from jax.experimental.pallas import tpu as pltpu
from jax.sharding import PartitionSpec as P

RANK = 32
VMEM_LIMIT = 32 * 1024 * 1024
HIGHEST = lax.Precision.HIGHEST
WHOLE = pl.BlockSpec(memory_space=pltpu.VMEM)
SCALARS = pl.BlockSpec(memory_space=pltpu.SMEM)
FAR = pl.BlockSpec(memory_space=pltpu.HBM)


def in_hbm(array):
    return pltpu.with_memory_space_constraint(array, pltpu.HBM)


def params():
    return pltpu.CompilerParams(vmem_limit_bytes=VMEM_LIMIT)


def mm(a, b, dims=((1,), (0,)), precision=None):
    return lax.dot_general(a, b, (dims, ((), ())), precision=precision, preferred_element_type=jnp.float32)


def iota(shape, axis):
    return lax.broadcasted_iota(jnp.int32, shape, axis)


def one_hot(condition):
    return jnp.where(condition, 1.0, 0.0).astype(jnp.bfloat16)


def group(count, rows, axis):
    index = iota((count, 1) if axis == 0 else (1, count), axis)
    if rows & (rows - 1) == 0:
        return jnp.right_shift(index, rows.bit_length() - 1), jnp.bitwise_and(index, rows - 1)
    return index // rows, index % rows


def spread_rows(rows):
    return one_hot(group(RANK * rows, rows, 0)[0] == iota((1, RANK), 1))


def same_place(tall, wide, rows):
    return group(tall, rows, 0)[1] == group(wide, rows, 1)[1]


def pick_rows(value, rows, j):
    tall = value.shape[0]
    return mm(one_hot(iota((1, tall), 1) == iota((tall // rows, 1), 0) * rows + j), value)


def padded_width(lon_count):
    return lon_count if lon_count % 128 == 0 else (lon_count + 2 + 127) // 128 * 128


def lon_shifts(value):
    return pltpu.roll(value, value.shape[1] - 1, 1), pltpu.roll(value, 1, 1)


def wrap_columns(ref, lon_count):
    width = ref.shape[1]
    if width != lon_count:
        ref[:, lon_count : lon_count + 1] = ref[:, 0:1]
        ref[:, width - 1 : width] = ref[:, lon_count - 1 : lon_count]


def bit_order(lat, bits):
    order = list(range(bits))
    if lat % 2 and bits > 1:
        order[0], order[1] = order[1], order[0]
    return order


def relative_place(tm, parity, bits):
    def place(order):
        total = 0
        for turn, bit in enumerate(order):
            total = total + (((tm >> bit) & 1) << (bits - 1 - turn))
        return total
    return jnp.where(parity == 1, place(bit_order(1, bits)), place(bit_order(0, bits)))


def places():
    bits = lax.axis_size("tm").bit_length() - 1
    tm, parity = lax.axis_index("tm"), jnp.bitwise_and(lax.axis_index("lat"), 1)
    return relative_place(tm, parity, bits), relative_place(tm, 1 - parity, bits)


def real_column(order, place):
    per_piece = RANK // lax.axis_size("tm")
    part, inner = group(RANK, per_piece, 0 if order.shape[1] == 1 else 1)
    if order.shape[0] * order.shape[1] != RANK:
        part, inner = order // per_piece, order % per_piece
    return jnp.bitwise_xor(part, place) * per_piece + inner


def cosine(row, total_rows):
    return jnp.cos((total_rows // 2 - row).astype(jnp.float32) * (jnp.pi / 720.0))


def weight(cosines):
    return 0.5 / jnp.sqrt(cosines)


def geometry(rows, repeat):
    total_rows = rows * lax.axis_size("lat")
    j = iota((rows, 1), 0)
    here = lax.axis_index("lat") * rows + j
    columns = [j] + [cosine(here + step, total_rows) for step in (-1, 0, 1)]
    return [jnp.concatenate([column] * repeat, axis=0) for column in columns]


def lat_shifts(value, rows):
    grouped = value.reshape(value.shape[0] // rows, rows, value.shape[1])
    return [pltpu.roll(grouped, by, 1).reshape(value.shape) for by in (1, rows - 1)]


def sketch_kernel(
    rows, lon_count, count_ref, ids_hbm, east_hbm, north_hbm, send_ref, keep_ref, up_near, up_far, down_near, down_far,
    signs_ref, ids, east, north, se, sw, sems
):
    slots = ids.shape[1]
    wide = RANK * rows
    cut = slots * rows // 32 * 16
    pieces = [pl.ds(0, cut), pl.ds(cut, slots * rows - cut)]
    keys = pltpu.make_async_copy(ids_hbm, ids, sems.at[4])
    keys.start()
    copies = []
    for source, target in ((east_hbm, east), (north_hbm, north)):
        for at in pieces:
            copy = pltpu.make_async_copy(source.at[at], target.at[at], sems.at[len(copies)])
            copy.start()
            copies.append(copy)
    me, beside = places()
    column = real_column(iota((RANK, 1), 0), me)
    spread = spread_rows(rows)
    across = one_hot(group(slots * rows, rows, 1)[0] == iota((slots, 1), 0))
    j, c_north, c_here, c_south = geometry(rows, 4)
    scale = weight(c_here)
    above_scale = jnp.where(j == 0, 0.0, -c_north * scale)
    below_scale = jnp.where(j == rows - 1, 0.0, c_south * scale)
    keys.wait()
    mixed = ids[...] * 1103515245 + (column * 40503 + 12345)
    mixed = jnp.bitwise_xor(mixed, jnp.right_shift(mixed, 13))
    mixed = mixed * 1664525 + 1013904223
    mixed = jnp.bitwise_xor(mixed, jnp.right_shift(mixed, 16))
    flipped = jnp.bitwise_and(jnp.right_shift(mixed, 7), 1)
    used = iota((1, slots), 1) < count_ref[0]
    signs = jnp.where(used, 1 - 2 * flipped, 0).astype(jnp.float32).astype(jnp.bfloat16)
    full = mm(mm(spread, signs).astype(jnp.bfloat16), across)
    signs_ref[...] = jnp.where(same_place(wide, slots * rows, rows), full, 0.0).astype(jnp.bfloat16)
    copies[0].wait()
    se[:, :lon_count] = mm(signs_ref[:, :cut], east[:cut, :])
    copies[1].wait()
    se[:, :lon_count] += mm(signs_ref[:, cut:], east[cut:, :])
    rounded = se[:, :lon_count].astype(jnp.bfloat16)
    order = real_column(iota((RANK, 1), 0), beside)
    tall_part, tall_place = group(wide, rows, 1)
    per_piece = RANK // lax.axis_size("tm")
    own = group(wide, rows * per_piece, 1)[0]
    own = jnp.bitwise_xor(own, me) * per_piece + (tall_part - own * per_piece)
    for row, near, far in ((rows - 1, up_near, up_far), (0, down_near, down_far)):
        edge = mm(one_hot((order == own) & (tall_place == row)), rounded).astype(jnp.bfloat16)
        near[...] = edge[: RANK // 2]
        far[...] = edge[RANK // 2 :]
    copies[2].wait()
    sw[:, :lon_count] = mm(signs_ref[:, :cut], north[:cut, :])
    copies[3].wait()
    sw[:, :lon_count] += mm(signs_ref[:, cut:], north[cut:, :])
    wrap_columns(sw, lon_count)
    band = 4 * rows
    for index in range(wide // band):
        at = slice(index * band, (index + 1) * band)
        ahead, behind = lon_shifts(sw[at, :])
        above, below = lat_shifts(se[at, :lon_count], rows)
        total = ((ahead - behind) * scale)[:, :lon_count] + above * above_scale + below * below_scale
        if index * band < wide // 2:
            keep_ref[at, :] = total
        else:
            send_ref[index * band - wide // 2 : (index + 1) * band - wide // 2, :] = total.astype(jnp.bfloat16)


def halo_kernel(rows, keep_ref, got_ref, up_near, up_far, down_near, down_far, send_ref, held_ref):
    tall = keep_ref.shape[0]
    edge_rows = tall // rows
    part, j = group(tall, rows, 0)
    source, column = group(4 * edge_rows, edge_rows, 1)
    goes = jnp.where(source < 2, 0, rows - 1)
    place = one_hot((part == column) & (j == goes))
    j, c_north, c_here, c_south = geometry(rows, 1)
    scale = weight(c_here) * jnp.where(j == 0, -c_north, c_south)
    scale = jnp.concatenate([scale] * edge_rows, axis=0)
    edges = jnp.concatenate([up_near[...], up_far[...], down_near[...], down_far[...]], axis=0)
    total = keep_ref[...] + got_ref[...].astype(jnp.float32) + scale * mm(place, edges)
    held_ref[...] = total[: tall // 2]
    send_ref[...] = total[tall // 2 :].astype(jnp.bfloat16)


def stencil_adjoint(rows, lon_count, work, to_east, to_north):
    band = 4 * rows
    j, c_north, c_here, c_south = geometry(rows, 4)
    scale = weight(c_here)
    above_scale = jnp.where(j == 0, 0.0, c_here * weight(c_north))
    below_scale = jnp.where(j == rows - 1, 0.0, -c_here * weight(c_south))
    for index in range(work.shape[0] // band):
        at = slice(index * band, (index + 1) * band)
        value = work[at, :]
        ahead, behind = lon_shifts(value)
        to_north[at, :] = ((behind - ahead) * scale)[:, :lon_count].astype(jnp.bfloat16)
        above, below = lat_shifts(value, rows)
        to_east[at, :] = (above * above_scale + below * below_scale)[:, :lon_count].astype(jnp.bfloat16)


def project_kernel(rows, lon_count, piece_ref, up_ref, down_ref, east_ref, north_ref, terms_ref, work, to_east, to_north):
    tall = piece_ref.shape[0]
    columns = tall // rows
    value = piece_ref[...]
    work[:, :lon_count] = value.astype(jnp.float32)
    wrap_columns(work, lon_count)
    stencil_adjoint(rows, lon_count, work, to_east, to_north)
    both = mm(east_ref[...], to_east[...], ((1,), (1,))) + mm(north_ref[...], to_north[...], ((1,), (1,)))
    slots = both.shape[0] // rows
    both = jnp.where(same_place(both.shape[0], tall, rows), both, 0.0)
    both = jnp.sum(both.reshape(slots, rows, tall), axis=1)
    fold = jnp.where(group(tall, rows, 1)[0] == iota((columns, 1), 0), 1.0, 0.0)
    terms = mm(fold, both, ((1,), (1,)), HIGHEST)
    total_rows = rows * lax.axis_size("lat")
    top = jnp.full((1, 1), lax.axis_index("lat") * rows, jnp.int32)
    first_scale = -cosine(top - 1, total_rows) * weight(cosine(top, total_rows))
    last_scale = cosine(top + rows, total_rows) * weight(cosine(top + rows - 1, total_rows))
    first = pick_rows(value, rows, 0) * first_scale
    last = pick_rows(value, rows, rows - 1) * last_scale
    terms += mm(first.astype(jnp.bfloat16), up_ref[...], ((1,), (1,)))
    terms += mm(last.astype(jnp.bfloat16), down_ref[...], ((1,), (1,)))
    terms_ref[...] = jnp.zeros_like(terms_ref)
    terms_ref[:, : terms.shape[1]] = terms


def gather_kernel(rows, piece_rows, first_ref, second_ref, head_ref, tail_ref, sketch_ref, sums_ref):
    wide = RANK * rows
    me, _ = places()
    start = 0
    for ref in (first_ref, second_ref):
        for inner in range(ref.shape[0] // piece_rows):
            owner = jnp.bitwise_xor(me, start)
            at = pl.ds(pl.multiple_of(owner * piece_rows, piece_rows), piece_rows)
            sketch_ref[at, :] = ref[inner * piece_rows : (inner + 1) * piece_rows, :]
            start += 1
    value = sketch_ref[...]
    fold = jnp.where(group(wide, rows, 1)[0] == iota((RANK, 1), 0), 1.0, 0.0)
    gram = jnp.where(same_place(wide, wide, rows), mm(value, value, ((1,), (1,))), 0.0)
    gram = mm(jnp.sum(gram.reshape(RANK, rows, wide), axis=1), fold, ((1,), (1,)), HIGHEST)
    turn = jnp.where(iota((RANK, 1), 0) == real_column(iota((1, RANK), 1), me), 1.0, 0.0)
    half = RANK // 2
    terms = mm(turn, jnp.concatenate([head_ref[...], tail_ref[...]], axis=0), precision=HIGHEST)
    offset = sums_ref.shape[1] - 128
    sums_ref[:, :offset] = terms
    sums_ref[:, offset:] = jnp.zeros((RANK, 128), jnp.float32)
    sums_ref[:, offset : offset + RANK] = gram


def eliminate(table, block):
    down = iota((table.shape[0], 1), 0)
    for k in range(0, RANK, block):
        columns = [jnp.broadcast_to(table[:, k + i : k + i + 1], table.shape) for i in range(block)]
        lines = [table[k + i : k + i + 1, :] for i in range(block)]
        for i in range(block):
            inverse = 1.0 / columns[i][k + i : k + i + 1, :]
            for m in range(i + 1, block):
                ratio = columns[m][k + i : k + i + 1, :] * inverse
                lines[m] = lines[m] - ratio * lines[i]
                columns[m] = columns[m] - ratio * columns[i]
            table = table - jnp.where(down > k + i, columns[i] * inverse, 0.0) * lines[i]
    return table


def solve_kernel(rows, cell_total, count_ref, sums_ref, sketch_ref, basis_ref, coeffs_ref, work):
    scale = 1.0 / cell_total
    slots = coeffs_ref.shape[1]
    wide = RANK * rows
    offset = sums_ref.shape[1] - 128
    work[...] = jnp.where(iota(work.shape, 0) + RANK == iota(work.shape, 1), 1.0, 0.0)
    work[:, :RANK] = sums_ref[:, offset : offset + RANK] * scale
    table = eliminate(work[...], 4)
    diagonal = jnp.sum(jnp.where(iota((RANK, 1), 0) == iota((1, 128), 1), table, 0.0), axis=1, keepdims=True)
    work[...] = table * (1.0 / jnp.sqrt(diagonal))
    inverse = work[:, RANK : 2 * RANK]
    spread = spread_rows(rows)
    same = same_place(wide, wide, rows)
    high = inverse.astype(jnp.bfloat16)
    rest = inverse - high.astype(jnp.float32)
    middle = rest.astype(jnp.bfloat16)
    value = sketch_ref[...]

    def apply(part):
        tall = mm(spread, part).astype(jnp.bfloat16)
        large = jnp.where(same, mm(tall, spread, ((1,), (1,))), 0.0).astype(jnp.bfloat16)
        return mm(large, value)

    basis_ref[...] = (apply(high) + apply(middle)).astype(jnp.bfloat16)
    raw = mm(inverse, sums_ref[:, :slots], precision=HIGHEST) * scale
    coeffs_ref[...] = jnp.where(iota((1, slots), 1) < count_ref[0], raw, 0.0)


def partners(turn, bits, tm_count, lat_count):
    pairs = []
    for tm in range(tm_count):
        for lat in range(lat_count):
            bit = bit_order(lat, bits)[turn]
            pairs.append((tm * lat_count + lat, (tm ^ (1 << bit)) * lat_count + lat))
    return pairs


def edge_pairs(step, far, bits, tm_count, lat_count):
    pairs = []
    for tm in range(tm_count):
        for lat in range(lat_count):
            target = lat + step
            if 0 <= target < lat_count:
                other = tm ^ (1 << bit_order(target, bits)[0]) if far else tm
                pairs.append((tm * lat_count + lat, other * lat_count + target))
    return pairs


def local(wind_east, wind_north, snap_counts, snap_ids):
    slots, rows, lon_count = wind_east.shape
    tm_count, lat_count = lax.axis_size("tm"), lax.axis_size("lat")
    bits = tm_count.bit_length() - 1
    wide = RANK * rows
    cell_total = rows * lat_count * lon_count
    width = padded_width(lon_count)
    east = wind_east.reshape(slots * rows, lon_count)
    north = wind_north.reshape(slots * rows, lon_count)
    both = ("tm", "lat")
    float_array = lambda *shape: jax.ShapeDtypeStruct(shape, jnp.float32)
    half_array = lambda *shape: jax.ShapeDtypeStruct(shape, jnp.bfloat16)

    outputs = pl.pallas_call(
        functools.partial(sketch_kernel, rows, lon_count),
        in_specs=[SCALARS, FAR, FAR, FAR],
        out_specs=[WHOLE] * 6,
        out_shape=[half_array(wide // 2, lon_count), float_array(wide // 2, lon_count)]
        + [half_array(RANK // 2, lon_count)] * 4,
        scratch_shapes=[
            pltpu.VMEM((wide, slots * rows), jnp.bfloat16),
            pltpu.VMEM((1, slots), jnp.int32),
            pltpu.VMEM((slots * rows, lon_count), jnp.bfloat16),
            pltpu.VMEM((slots * rows, lon_count), jnp.bfloat16),
            pltpu.VMEM((wide, width), jnp.float32),
            pltpu.VMEM((wide, width), jnp.float32),
            pltpu.SemaphoreType.DMA((5,)),
        ],
        compiler_params=params(),
        name="sketch_terms",
    )(snap_counts, in_hbm(snap_ids.reshape(1, slots)), in_hbm(east), in_hbm(north))
    send, keep, up_near, up_far, down_near, down_far = outputs

    got = lax.ppermute(send, both, partners(0, bits, tm_count, lat_count))
    edges = [
        lax.ppermute(up_near, both, edge_pairs(1, False, bits, tm_count, lat_count)),
        lax.ppermute(up_far, both, edge_pairs(1, True, bits, tm_count, lat_count)),
        lax.ppermute(down_near, both, edge_pairs(-1, False, bits, tm_count, lat_count)),
        lax.ppermute(down_far, both, edge_pairs(-1, True, bits, tm_count, lat_count)),
    ]
    send, keep = pl.pallas_call(
        functools.partial(halo_kernel, rows),
        in_specs=[WHOLE] * 6,
        out_specs=[WHOLE, WHOLE],
        out_shape=[half_array(wide // 4, lon_count), float_array(wide // 4, lon_count)],
        compiler_params=params(),
        name="halo_terms",
    )(keep, got, *edges)

    edge_source, send = lax.optimization_barrier((wind_east, send))
    wind_above = lax.ppermute(edge_source[:, rows - 1, :], both, edge_pairs(1, False, bits, tm_count, lat_count))
    wind_below = lax.ppermute(edge_source[:, 0, :], both, edge_pairs(-1, False, bits, tm_count, lat_count))

    for turn in range(1, bits):
        got = lax.ppermute(send, both, partners(turn, bits, tm_count, lat_count))
        if turn == bits - 1:
            got, wind_above, wind_below = lax.optimization_barrier((got, wind_above, wind_below))
        keep = keep + got.astype(jnp.float32)
        if turn < bits - 1:
            half = keep.shape[0] // 2
            send, keep = keep[half:].astype(jnp.bfloat16), keep[:half]
    held = keep.astype(jnp.bfloat16)
    piece_rows = held.shape[0]
    for turn in reversed(range(1, bits)):
        got = lax.ppermute(held, both, partners(turn, bits, tm_count, lat_count))
        held = jnp.concatenate([held, got], axis=0)
    got = lax.ppermute(held, both, partners(0, bits, tm_count, lat_count))

    terms_width = -(-slots // 128) * 128

    def project(piece):
        tall = piece.shape[0]
        return pl.pallas_call(
            functools.partial(project_kernel, rows, lon_count),
            in_specs=[WHOLE] * 5,
            out_specs=WHOLE,
            out_shape=float_array(tall // rows, terms_width),
            scratch_shapes=[
                pltpu.VMEM((tall, width), jnp.float32),
                pltpu.VMEM((tall, lon_count), jnp.bfloat16),
                pltpu.VMEM((tall, lon_count), jnp.bfloat16),
            ],
            cost_estimate=pl.CostEstimate(
                flops=4 * tall * slots * rows * lon_count,
                bytes_accessed=4 * slots * rows * lon_count,
                transcendentals=0,
            ),
            compiler_params=params(),
            name="projection_terms",
        )(piece, wind_above, wind_below, east, north)

    head, tail = project(held), project(got)
    sketch, sums = pl.pallas_call(
        functools.partial(gather_kernel, rows, piece_rows),
        in_specs=[WHOLE] * 4,
        out_specs=[WHOLE, WHOLE],
        out_shape=[half_array(wide, lon_count), float_array(RANK, terms_width + 128)],
        compiler_params=params(),
        name="gram_terms",
    )(held, got, head, tail)

    shift = 1
    while shift < lat_count:
        sums = sums + lax.ppermute(sums, "lat", [(i, i ^ shift) for i in range(lat_count)])
        shift *= 2

    basis, coeffs = pl.pallas_call(
        functools.partial(solve_kernel, rows, cell_total),
        in_specs=[SCALARS, WHOLE, WHOLE],
        out_specs=[WHOLE, WHOLE],
        out_shape=[half_array(wide, lon_count), float_array(RANK, slots)],
        scratch_shapes=[pltpu.VMEM((RANK, 128), jnp.float32)],
        compiler_params=params(),
        name="basis_and_coeffs",
    )(snap_counts, sums, sketch)
    return basis.reshape(RANK, rows, lon_count), coeffs


def solution(mesh):
    in_specs = (P("tm", "lat", None), P("tm", "lat", None), P("tm"), P("tm"))
    out_specs = (P(None, "lat", None), P(None, "tm"))
    return jax.shard_map(local, mesh=mesh, in_specs=in_specs, out_specs=out_specs, check_vma=False)
```
